512 devices in a mesh: users: 64 (over y, z_hi, x), cand: 8 (over z_lo, core).
Axes of the slice: x: 4, y: 8, z: 8 (z_hi: 2, z_lo: 4; z = z_hi * 4 + z_lo), core: 2. Of those that a mesh axis runs over, the one named last changes fastest.
Arguments:
- candidate_rows: bfloat16 [32768, 1024], P(('users', 'cand')), may hold values from -6 to 6
- weight_in: bfloat16 [2, 1024, 8, 512], P(None, None, 'cand'), may hold values from -0.1875 to 0.1875
- weight_out: bfloat16 [2, 8, 128, 1024], P(None, 'cand'), may hold values from -0.1875 to 0.1875
- history_cache: bfloat16 [2, 2, 8192, 8, 128], P(None, None, 'users', 'cand'), may hold values from -6 to 6
- block_user: int32 [64], replicated, may hold values from 0 to 15, as said below
- block_offset: int32 [64], replicated, may hold values from 0 to 31, as said below
- history_length: int32 [16], replicated, may hold values from 1 to 4096, as said below
- candidate_count: int32 [16], replicated, may hold values from 1 to 16384, as said below
Outputs:
- scored_rows: bfloat16 [32768, 1024], P(('users', 'cand'))
The draws below stay inside these ranges and needn't reach their ends.
Inputs may be any that keep to these rules, and one draw needn't show every extreme that they name: `block_user`: every one of the 16 users owns at least one block; the blocks of one user may stand anywhere; exactly one user owns 64 / 2 blocks, every other user fewer. `block_offset`: the blocks of a user that owns b blocks carry the offsets 0 to b - 1, each once. `history_length`: a user that owns b blocks has more than (b - 1) * 128 and at most b * 128 history rows. `candidate_count`: the counts sum to 32768; the rows of one user are consecutive, users in increasing order.
All inputs are finite; a program needn't handle non-finite values.
Results may differ from the reference program's by a relative error of at most 0.027.
Values may be sent and summed in bfloat16 or wider, within the bound.
A program may use at most 64 MiB of HBM per device.

```python
import math
import jax
import jax.numpy as jnp
from jax import lax

D = 1024
HEADS = 8
DH = 128
LAYERS = 2
BLOCK = 128
NU = 16
NBLK = 64
NROWS = 8192
CAND = 32768
N_CAND = 8


def split_points(key, total, pieces):
    cut_points = jnp.sort(jax.random.permutation(key, total - 1)[:pieces - 1].astype(jnp.int32) + 1)
    boundaries = jnp.concatenate([jnp.zeros((1,), jnp.int32), cut_points, jnp.full((1,), total, jnp.int32)])
    return boundaries


def heavy_split(key, total, pieces):
    heavy_key, rest_key = jax.random.split(key, 2)
    heavy_size = total // 2
    heavy_user = jax.random.randint(heavy_key, (), 0, pieces).astype(jnp.int32)
    rest_bounds = split_points(rest_key, total - heavy_size, pieces - 1)
    others = rest_bounds[1:] - rest_bounds[:-1]
    users_all = jnp.arange(pieces, dtype=jnp.int32)
    below = others[jnp.clip(users_all, 0, pieces - 2)]
    above = others[jnp.clip(users_all - 1, 0, pieces - 2)]
    sizes = jnp.where(users_all < heavy_user, below, jnp.where(users_all == heavy_user, heavy_size, above)).astype(jnp.int32)
    return (sizes, heavy_user)


def history_plan(key):
    folded = jax.random.fold_in(key, 7)
    cut_key, order_key, tail_key = jax.random.split(folded, 3)
    per_user, heavy_user = heavy_split(cut_key, NBLK, NU)
    boundaries = jnp.concatenate([jnp.zeros((1,), jnp.int32), jnp.cumsum(per_user).astype(jnp.int32)])
    cut_points = boundaries[1:-1]
    sorted_ids = jnp.arange(NBLK, dtype=jnp.int32)
    owner_sorted = jnp.sum((sorted_ids[:, None] >= cut_points[None, :]).astype(jnp.int32), axis=1)
    offset_sorted = sorted_ids - boundaries[owner_sorted]
    shuffle = jax.random.permutation(order_key, NBLK)
    owners = owner_sorted[shuffle]
    offsets = offset_sorted[shuffle]
    tail_rows = jax.random.randint(tail_key, (NU,), 1, BLOCK + 1).astype(jnp.int32)
    tail_rows = jnp.where(jnp.arange(NU, dtype=jnp.int32) == heavy_user, BLOCK, tail_rows)
    lengths = (per_user - 1) * BLOCK + tail_rows
    return (owners, offsets, lengths)


def draw_block_user(key, part):
    return history_plan(key)[0]


def draw_block_offset(key, part):
    return history_plan(key)[1]


def draw_history_length(key, part):
    return history_plan(key)[2]


def draw_candidate_count(key, part):
    folded = jax.random.fold_in(key, 23)
    sizes, heavy_user = heavy_split(folded, CAND, NU)
    return sizes


def shard_levels(stream_key, extent, shards, least, top_value):
    gain = 1.0
    for axis_at, parts in shards:
        heights = jax.random.uniform(jax.random.fold_in(jax.random.fold_in(stream_key, 6), axis_at), (parts,), jnp.float32, least / len(shards), top_value / len(shards))
        gain = gain * jnp.repeat(jnp.exp(heights), extent[axis_at] // parts).reshape((-1,) + (1,) * (len(extent) - 1 - axis_at))
    return gain


def gaussian(key, dims, spread, limit, shards=(), kind=jnp.bfloat16):
    level = shard_levels(key, dims, shards, -0.22, 0.18) if shards else 1.0
    array = jax.random.normal(key, dims, jnp.float32) * spread * level
    return jnp.minimum(jnp.maximum(array, -limit), limit).astype(kind)


def setup_inputs(seed: int = 0) -> dict:
    streams_of = jax.random.split(jax.random.key(seed), 9)
    candidate_rows = gaussian(streams_of[0], (CAND, D), 1.0, 6.0, ((0, 512),))
    weight_in = gaussian(streams_of[1], (LAYERS, D, HEADS, 4 * DH), D ** -0.5, 0.1875, ((2, 8),))
    weight_out = gaussian(streams_of[2], (LAYERS, HEADS, DH, D), (HEADS * DH) ** -0.5, 0.1875, ((1, 8),))
    history_cache = gaussian(streams_of[3], (LAYERS, 2, NROWS, HEADS, DH), 1.0, 6.0, ((2, 64), (3, 8)))
    block_user = draw_block_user(jax.random.fold_in(streams_of[8], 71), 0)
    block_offset = draw_block_offset(jax.random.fold_in(streams_of[8], 71), 0)
    history_length = draw_history_length(jax.random.fold_in(streams_of[8], 71), 0)
    candidate_count = draw_candidate_count(jax.random.fold_in(streams_of[8], 71), 0)
    return {"candidate_rows": candidate_rows, "weight_in": weight_in, "weight_out": weight_out, "history_cache": history_cache, "block_user": block_user, "block_offset": block_offset, "history_length": history_length, "candidate_count": candidate_count}


def reference(candidate_rows, weight_in, weight_out, history_cache, block_user, block_offset, history_length, candidate_count):
    score_scale = 1.0 / math.sqrt(DH)
    user_ends = jnp.cumsum(candidate_count)
    cand_user = lax.optimization_barrier(jnp.sum((jnp.arange(CAND, dtype=jnp.int32)[:, None] >= user_ends[None, :]).astype(jnp.int32), axis=1))
    users_all = jnp.arange(NU, dtype=jnp.int32)
    row_place = block_offset[:, None] * BLOCK + jnp.arange(BLOCK, dtype=jnp.int32)[None, :]
    owner_length = lax.optimization_barrier(jnp.sum(jnp.where(block_user[:, None] == users_all[None, :], history_length[None, :], 0), axis=1))
    row_valid = row_place < owner_length[:, None]
    cand_block = 512 if CAND % 512 == 0 else CAND
    group_width = HEADS // N_CAND * DH
    current = candidate_rows
    for layer_index in range(LAYERS):
        flat = weight_in[layer_index].reshape(D, HEADS * 4 * DH)
        mixed = jnp.dot(current, flat, preferred_element_type=jnp.float32)
        projected = jax.nn.silu(mixed).astype(jnp.bfloat16).reshape(CAND, HEADS, 4, DH)
        gate_part = projected[:, :, 0]
        values_part = projected[:, :, 1]
        queries = projected[:, :, 2]
        keys_part = projected[:, :, 3]
        key_blocks = history_cache[layer_index, 0].reshape(NBLK, BLOCK, HEADS, DH)
        value_blocks = history_cache[layer_index, 1].reshape(NBLK, BLOCK, HEADS, DH)

        def attend_group(inputs):
            query_group, user_group = inputs

            def visit_block(running, block_inputs):
                key_block, value_block, block_owner, valid_rows = block_inputs
                visible = (user_group[:, None] == block_owner) & valid_rows[None, :]

                def compute(running_sum):
                    scores = jnp.einsum('rhd,nhd->hrn', query_group.astype(jnp.float32), key_block.astype(jnp.float32)) * score_scale
                    weights = jnp.where(visible[None], jax.nn.silu(scores), 0.0).astype(jnp.bfloat16)
                    return running_sum + jnp.einsum('hrn,nhd->rhd', weights.astype(jnp.float32), value_block.astype(jnp.float32))

                def unchanged(running_sum):
                    return running_sum
                return (lax.cond(jnp.any(visible), compute, unchanged, running), None)
            initial = jnp.zeros((cand_block, HEADS, DH), jnp.float32)
            result, unused = lax.scan(visit_block, initial, (key_blocks, value_blocks, block_user, row_valid))
            return result
        attended = lax.map(attend_group, (queries.reshape(CAND // cand_block, cand_block, HEADS, DH), cand_user.reshape(CAND // cand_block, cand_block)))
        attended = attended.reshape(CAND, HEADS, DH)
        own_score = lax.optimization_barrier(jnp.sum(queries.astype(jnp.float32) * keys_part.astype(jnp.float32), axis=-1)) * score_scale
        own_weight = jax.nn.silu(own_score).astype(jnp.bfloat16)
        attended = attended + own_weight.astype(jnp.float32)[..., None] * values_part.astype(jnp.float32)
        centred = attended - lax.optimization_barrier(jnp.mean(attended, axis=-1, keepdims=True))
        variance = lax.optimization_barrier(jnp.mean(centred * centred, axis=-1, keepdims=True))
        gated = (centred * lax.rsqrt(variance + 1e-05) * gate_part.astype(jnp.float32)).astype(jnp.bfloat16)
        gated_flat = gated.reshape(CAND, HEADS * DH)
        out_flat = weight_out[layer_index].reshape(HEADS * DH, D)
        total = current.astype(jnp.float32)
        for group_index in range(N_CAND):
            group_in = gated_flat[:, group_index * group_width:(group_index + 1) * group_width]
            group_weight = out_flat[group_index * group_width:(group_index + 1) * group_width]
            group_term = jnp.dot(group_in, group_weight, preferred_element_type=jnp.float32).astype(jnp.bfloat16)
            group_term = lax.optimization_barrier(group_term)
            total = total + group_term.astype(jnp.float32)
        current = total.astype(jnp.bfloat16)
    return current
```

```python
import math

import jax
import jax.numpy as jnp
from jax import lax
from jax.experimental import pallas as pl
from jax.experimental.pallas import tpu as pltpu
from jax.sharding import PartitionSpec as P

BLOCK = 128
NX, NY, NZ, NC = 4, 8, 2, 8
ROWS_A, ROWS_B = 48, 80
OWN, D, DH, USERS = 64, 1024, 128, 16
GROUP = OWN * NC
HIDE = -1e30
CHUNKS = 2
MESSAGES = 200
SCALE = 1.0 / math.sqrt(DH)


def half_silu(h):
    return h * jnp.tanh(h) + h


def kernel(
    x_ref, win_ref, wout_ref, hist_ref, user_ref, place_ref, length_ref, count_ref, out_ref,
    kva, kvb, ma, mb, xg, x1, win, wout, qp, gate, acc, gat, gown, g1,
    send_sem, recv_sem, local_sem,
):
    u, c = lax.axis_index("users"), lax.axis_index("cand")
    y, zh, x = u // 8, (u // 4) % 2, u % 4
    zl, core = c // 2, c % 2
    sib = zl * 2 + (1 - core)

    def at(y_, zh_, x_):
        return y_ * 8 + zh_ * 4 + x_

    xs = [(x + k) % NX for k in range(NX)]
    ys = [(y + k) % NY for k in range(NY)]
    right, left = (at(y, zh, xs[1]), c), (at(y, zh, xs[3]), c)
    up, down = (at(ys[1], zh, x), c), (at(ys[7], zh, x), c)
    over = (at(y, 1 - zh, x), c)
    z8 = zh * 4 + zl
    zu, zd = (z8 + 1) % 8, (z8 + 7) % 8
    ring_up = (at(y, zu // 4, x), (zu % 4) * 2 + core)
    ring_down = (at(y, zd // 4, x), (zd % 4) * 2 + core)
    zls = [(zl + k) % 4 for k in range(4)]

    def line(k):
        return (u, zls[k] * 2 + core)

    local = []

    def fetch(src, dst):
        copy = pltpu.make_async_copy(src, dst, local_sem.at[len(local)])
        copy.start()
        local.append(copy)
        return copy

    first = [fetch(x_ref, xg.at[c])]
    for l in range(2):
        first.append(fetch(hist_ref.at[l, :, pl.ds(0, ROWS_A)], kva.at[l, zh, y, x]))
        first.append(fetch(hist_ref.at[l, :, pl.ds(ROWS_A, ROWS_B)], kvb.at[l, zh, x, y]))
    second = [fetch(wout_ref.at[l], wout.at[l, c]) for l in range(2)]
    third = [fetch(win_ref.at[l], win.at[l]) for l in range(2)]

    barrier = pltpu.get_barrier_semaphore()
    friends = [right, left, up, down, over, ring_up, ring_down]
    friends += [(u, (c + k) % NC) for k in range(1, NC)]
    for friend in friends:
        pl.semaphore_signal(barrier, inc=1, device_id=friend, device_id_type=pl.DeviceIdType.MESH)
    pl.semaphore_wait(barrier, len(friends))

    sent = []

    def send(src, dst, to):
        n = len(sent)
        copy = pltpu.make_async_remote_copy(
            src_ref=src, dst_ref=dst, send_sem=send_sem.at[n], recv_sem=recv_sem.at[n],
            device_id=to, device_id_type=pl.DeviceIdType.MESH,
        )
        copy.start()
        sent.append(copy)
        return copy

    def same(ref, to):
        return send(ref, ref, to)

    def got(copies):
        for copy in copies:
            copy.wait_recv()

    class Chain:
        def __init__(self, l, z):
            self.l, self.z = l, z

        def a(self, yy, *rest):
            return kva.at[(self.l, self.z, yy) + rest]

        def b(self, xx, *rest):
            return kvb.at[(self.l, self.z, xx) + rest]

        def r0(self):
            s = self.a(y, x)
            self.ax = [same(s, right), same(s, left)]
            s = self.b(x, y)
            self.by = [same(s, up), same(s, down)]

        def r1(self):
            got(self.ax)
            self.ax = [same(self.a(y, xs[3], 0), right), same(self.a(y, xs[1], 1), left)]
            got(self.by)
            self.by = [same(self.b(x, ys[7]), up), same(self.b(x, ys[1]), down)]

        def r2(self):
            got(self.ax)
            s = self.a(y)
            self.ay = [same(s, up), same(s, down)]
            got(self.by)
            self.by = [same(self.b(x, ys[6]), up), same(self.b(x, ys[2]), down)]

        def r3(self):
            got(self.by)
            self.by = [same(self.b(x, ys[5], 0), up), same(self.b(x, ys[3], 1), down)]
            got(self.ay)
            self.ay = [same(self.a(ys[7]), up), same(self.a(ys[1]), down)]

        def r4(self):
            got(self.by)
            s = self.b(x)
            self.bx = [same(s, right), same(s, left)]
            got(self.ay)
            self.ay = [same(self.a(ys[6]), up), same(self.a(ys[2]), down)]

        def r5(self):
            got(self.ay)
            self.ay = [
                same(self.a(ys[5], pl.ds(0, 2)), up),
                same(self.a(ys[3], pl.ds(2, 2)), down),
            ]

        def r6(self):
            got(self.ay)

        def r7(self):
            got(self.bx)
            self.bx = [
                same(self.b(xs[3], pl.ds(0, 4)), right),
                same(self.b(xs[1], pl.ds(4, 4)), left),
            ]

        def r8(self):
            got(self.bx)

    def scores(rows, k, m, v):
        s = lax.dot_general(
            qp[rows, :], jnp.concatenate([k, m], axis=1), (((1,), (1,)), ((), ())),
            preferred_element_type=jnp.float32,
        )
        w = half_silu(jnp.maximum(s * (0.5 * SCALE), -100.0)).astype(jnp.bfloat16)
        acc[rows, :] += jnp.dot(w, v, preferred_element_type=jnp.float32)

    def attend_a(l, offsets):
        low, step = offsets[0], (offsets[1] - offsets[0]) if len(offsets) > 1 else 1

        @pl.loop(0, 2 * len(offsets))
        def _(i):
            yy = (y + low + (i // 2) * step) % NY
            rows = pl.ds(pl.multiple_of((i % 2) * 256, 256), 256)
            n = NZ * NX * ROWS_A
            scores(
                rows,
                kva[l, :, yy, :, 0].reshape(n, DH),
                ma[:, yy].reshape(n, DH),
                kva[l, :, yy, :, 1].reshape(n, DH),
            )

    def attend_b(l, chunks):
        where, number = chunks

        @pl.loop(0, 2 * number)
        def _(i):
            zz, xx = where(i // 2)
            rows = pl.ds(pl.multiple_of((i % 2) * 256, 256), 256)
            n = NY * ROWS_B
            scores(
                rows,
                kvb[l, zz, xx, :, 0].reshape(n, DH),
                mb[zz, xx].reshape(n, DH),
                kvb[l, zz, xx, :, 1].reshape(n, DH),
            )

    def project(l, rows, value):
        mixed = jnp.dot(value, win[l], preferred_element_type=jnp.float32)
        p = half_silu(0.5 * mixed).astype(jnp.bfloat16)
        q = p[:, 2 * DH:3 * DH]
        gate[rows, :] = p[:, :DH]
        qp[rows, pl.ds(0, DH)] = q
        own = jnp.sum(
            q.astype(jnp.float32) * p[:, 3 * DH:].astype(jnp.float32), axis=1, keepdims=True
        )
        own = half_silu(own * (0.5 * SCALE)).astype(jnp.bfloat16).astype(jnp.float32)
        acc[rows, :] = own * p[:, DH:2 * DH].astype(jnp.float32)

    def gated(rows):
        a = acc[rows, :]
        centred = a - jnp.mean(a, axis=1, keepdims=True)
        variance = jnp.mean(centred * centred, axis=1, keepdims=True)
        return (
            centred * lax.rsqrt(variance + 1e-05) * gate[rows, :].astype(jnp.float32)
        ).astype(jnp.bfloat16)

    class Weights:
        def __init__(self, l):
            self.l = l

        def slot(self, k):
            return zls[k % 4] * 2 + core

        def w1(self):
            s = wout.at[self.l, c]
            self.z = [same(s, ring_up), same(s, ring_down)]
            self.s = [same(s, (u, sib))]

        def w2(self):
            got(self.z)
            below, above = wout.at[self.l, self.slot(3)], wout.at[self.l, self.slot(1)]
            self.z = [
                same(below.at[pl.ds(0, 64)], ring_up), same(above.at[pl.ds(64, 64)], ring_down)
            ]
            self.s += [same(below, (u, sib)), same(above, (u, sib))]

        def w3(self):
            got(self.z)
            self.s += [same(wout.at[self.l, self.slot(2)], (u, sib))]

        def w4(self):
            got(self.s)

    for copy in first:
        copy.wait()
    xsend = [same(xg.at[c], line(k)) for k in range(1, 4)]
    xshare = [same(xg.at[c], (u, sib))]
    across = []
    for l in range(2):
        across.append([same(kva.at[l, zh, y, x], over), same(kvb.at[l, zh, x, y], over)])
        if l == 0:
            chains = [[Chain(i, zh), Chain(i, 1 - zh)] for i in range(2)]
            o, p = chains[0]
            o.r0()
    o1, p1 = chains[1]
    w0, w1 = Weights(0), Weights(1)

    lane = lax.broadcasted_iota(jnp.int32, (BLOCK, BLOCK), 1)
    sub = lax.broadcasted_iota(jnp.int32, (BLOCK, BLOCK), 0)

    @pl.loop(0, NX * NY * NZ)
    def _(b):
        by, bz, bx = b // 8, (b // 4) % 2, b % 4
        owner = user_ref[b]
        valid = length_ref[owner] - place_ref[b] * BLOCK
        code = jnp.where(sub < valid, owner, USERS)
        hot = jnp.where(lane == code, 1.0, 0.0).astype(jnp.bfloat16)
        ma[bz, by, bx] = hot[:ROWS_A]
        mb[bz, bx, by] = hot[ROWS_A:]

    o.r1()

    @pl.loop(0, GROUP // BLOCK)
    def _(t):
        row = u * GROUP + t * BLOCK + sub
        end = count_ref[0]
        cu = (row >= end).astype(jnp.int32)
        for k in range(1, USERS):
            end = end + count_ref[k]
            cu = cu + (row >= end).astype(jnp.int32)
        hide = jnp.where((lane == cu) | (lane > USERS), 0.0, HIDE)
        qp[pl.ds(pl.multiple_of(t * BLOCK, BLOCK), BLOCK), pl.ds(DH, DH)] = hide.astype(jnp.bfloat16)

    got(across[0])
    p.r0()
    o.r2()
    p.r1()
    o.r3()
    for k in range(1, 4):
        got([xsend[k - 1]])
        xshare.append(same(xg.at[zls[4 - k] * 2 + core], (u, sib)))
    for copy in second:
        copy.wait()
    w0.w1()
    p.r2()
    o.r4()
    for copy in third:
        copy.wait()
    got(xshare)

    @pl.loop(0, 4)
    def _(t):
        part = pl.ds(pl.multiple_of(t * 2, 2), 2)
        rows = pl.ds(pl.multiple_of(t * BLOCK, BLOCK), BLOCK)
        project(0, rows, xg[part].reshape(BLOCK, D))

    p.r3()
    w0.w2()
    o.r5()
    p.r4()
    attend_a(0, [-1 + NY, NY, NY + 1])
    got(across[1])
    o1.r0()
    p1.r0()
    w0.w3()
    p.r5()
    o.r6()
    attend_a(0, [2, 6])
    o1.r1()
    p1.r1()
    p.r6()
    attend_b(0, (lambda i: (i, x), 2))
    o.r7()
    o1.r2()
    p1.r2()
    attend_a(0, [3, 4, 5])
    attend_b(0, (lambda i: (zh, (x + 1 + 2 * i) % NX), 2))
    p.r7()
    o1.r3()
    p1.r3()
    attend_b(0, (lambda i: (1 - zh, (x + 1 + 2 * i) % NX), 2))
    o.r8()
    w0.w4()
    o1.r4()
    p.r8()
    attend_b(0, (lambda i: (i, (x + 2) % NX), 2))

    size = GROUP // CHUNKS
    gsend, gshare = [], []
    for r in range(CHUNKS):
        rows = pl.ds(r * size, size)
        gat[c, rows] = gated(rows)
        gsend.append([same(gat.at[c, rows], line(k)) for k in range(1, 4)])
        gshare.append([same(gat.at[c, rows], (u, sib))])
    p1.r4()
    for r in range(CHUNKS):
        rows = pl.ds(r * size, size)
        for k in range(1, 4):
            got([gsend[r][k - 1]])
            gshare[r].append(same(gat.at[zls[4 - k] * 2 + core, rows], (u, sib)))
        if r == 0:
            o1.r5()
    w1.w1()
    p1.r5()
    for r in range(CHUNKS):
        got(gshare[r])

        @pl.loop(0, size // BLOCK)
        def _(t):
            first_row = r * size + t * BLOCK
            rows = pl.ds(pl.multiple_of(first_row, BLOCK), BLOCK)
            part = pl.ds(pl.multiple_of(r * (size // OWN) + t * 2, 2), 2)
            g = jnp.concatenate([gat[h, rows] for h in range(NC)], axis=1)
            term = jnp.dot(g, wout[0].reshape(D, D), preferred_element_type=jnp.float32)
            new = (xg[part].reshape(BLOCK, D).astype(jnp.float32) + term).astype(jnp.bfloat16)
            x1[rows, :] = new
            project(1, rows, new)

    w1.w2()
    o1.r6()
    o1.r7()
    p1.r6()
    p1.r7()
    attend_a(1, list(range(NY)))
    w1.w3()
    attend_b(1, (lambda i: (i % 2, (x + 3 + i // 2) % NX), 6))
    w1.w4()
    o1.r8()
    p1.r8()
    attend_b(1, (lambda i: (i, (x + 2) % NX), 2))
    gown[...] = gated(slice(None))
    back = []
    for k in range(1, NC):
        to = (c + k) % NC
        rows = pl.ds(pl.multiple_of(to * OWN, OWN), OWN)
        back.append(send(gown.at[rows], g1.at[c], (u, to)))
    mine = pl.ds(pl.multiple_of(c * OWN, OWN), OWN)
    g1[c] = gown[mine, :]
    got(back)
    g = jnp.concatenate([g1[h] for h in range(NC)], axis=1)
    term = jnp.dot(g, wout[1].reshape(D, D), preferred_element_type=jnp.float32)
    out_ref[...] = (x1[mine, :].astype(jnp.float32) + term).astype(jnp.bfloat16)
    for copy in sent:
        copy.wait_send()


def body(rows, weight_in, weight_out, cache, block_user, block_offset, length, count):
    bf16 = jnp.bfloat16
    hbm, smem = pl.BlockSpec(memory_space=pl.ANY), pl.BlockSpec(memory_space=pltpu.SMEM)
    return pl.pallas_call(
        kernel,
        out_shape=jax.ShapeDtypeStruct((OWN, D), bf16),
        in_specs=[hbm] * 4 + [smem] * 4,
        out_specs=pl.BlockSpec(memory_space=pltpu.VMEM),
        scratch_shapes=[
            pltpu.VMEM((2, NZ, NY, NX, 2, ROWS_A, DH), bf16),
            pltpu.VMEM((2, NZ, NX, NY, 2, ROWS_B, DH), bf16),
            pltpu.VMEM((NZ, NY, NX, ROWS_A, DH), bf16),
            pltpu.VMEM((NZ, NX, NY, ROWS_B, DH), bf16),
            pltpu.VMEM((NC, OWN, D), bf16),
            pltpu.VMEM((GROUP, D), bf16),
            pltpu.VMEM((2, D, 4 * DH), bf16),
            pltpu.VMEM((2, NC, DH, D), bf16),
            pltpu.VMEM((GROUP, 2 * DH), bf16),
            pltpu.VMEM((GROUP, DH), bf16),
            pltpu.VMEM((GROUP, DH), jnp.float32),
            pltpu.VMEM((NC, GROUP, DH), bf16),
            pltpu.VMEM((GROUP, DH), bf16),
            pltpu.VMEM((NC, OWN, DH), bf16),
            pltpu.SemaphoreType.DMA((MESSAGES,)),
            pltpu.SemaphoreType.DMA((MESSAGES,)),
            pltpu.SemaphoreType.DMA((9,)),
        ],
        compiler_params=pltpu.CompilerParams(
            collective_id=0, has_side_effects=True, vmem_limit_bytes=48 * 1024 * 1024
        ),
        cost_estimate=pl.CostEstimate(
            flops=12_000_000_000, bytes_accessed=4_000_000, transcendentals=9_000_000
        ),
    )(
        rows,
        weight_in.reshape(2, D, 4 * DH),
        weight_out.reshape(2, DH, D),
        cache.reshape(2, 2, BLOCK, DH),
        block_user,
        block_offset,
        length,
        count,
    )


def solution(mesh):
    placed = (
        P(("users", "cand"), None),
        P(None, None, "cand", None),
        P(None, "cand", None, None),
        P(None, None, "users", "cand", None),
        P(),
        P(),
        P(),
        P(),
    )
    return jax.shard_map(
        body, mesh=mesh, in_specs=placed, out_specs=P(("users", "cand"), None), check_vma=False
    )
```

```python
import math

import jax
import jax.numpy as jnp
from jax import lax
from jax.experimental import pallas as pl
from jax.experimental.pallas import tpu as pltpu
from jax.sharding import PartitionSpec as P

BLOCK = 128
NX, NY, NZ, NC = 4, 8, 2, 8
ROWS_A, ROWS_B = 48, 80
OWN, D, DH, USERS = 64, 1024, 128, 16
GROUP = OWN * NC
HIDE = -1e30
CHUNKS = 2
MESSAGES = 208
SCALE = 1.0 / math.sqrt(DH)


def half_silu(h):
    return h * jnp.tanh(h) + h


def kernel(
    x_ref, win_ref, wout_ref, hist_ref, user_ref, place_ref, length_ref, count_ref, out_ref,
    kva, kvb, ma, mb, xg, x1, win, wout, qp, gate, acc, gat, gown, g1,
    send_sem, recv_sem, local_sem,
):
    u, c = lax.axis_index("users"), lax.axis_index("cand")
    y, zh, x = u // 8, (u // 4) % 2, u % 4
    zl, core = c // 2, c % 2
    sib = zl * 2 + (1 - core)

    def at(y_, zh_, x_):
        return y_ * 8 + zh_ * 4 + x_

    xs = [(x + k) % NX for k in range(NX)]
    ys = [(y + k) % NY for k in range(NY)]
    right, left = (at(y, zh, xs[1]), c), (at(y, zh, xs[3]), c)
    up, down = (at(ys[1], zh, x), c), (at(ys[7], zh, x), c)
    over = (at(y, 1 - zh, x), c)
    z8 = zh * 4 + zl
    zu, zd = (z8 + 1) % 8, (z8 + 7) % 8
    ring_up = (at(y, zu // 4, x), (zu % 4) * 2 + core)
    ring_down = (at(y, zd // 4, x), (zd % 4) * 2 + core)
    zls = [(zl + k) % 4 for k in range(4)]

    def line(k):
        return (u, zls[k] * 2 + core)

    local = []

    def fetch(src, dst):
        copy = pltpu.make_async_copy(src, dst, local_sem.at[len(local)])
        copy.start()
        local.append(copy)
        return copy

    first = [fetch(x_ref, xg.at[c])]
    for l in range(2):
        first.append(fetch(hist_ref.at[l, :, pl.ds(0, ROWS_A)], kva.at[l, zh, y, x]))
        first.append(fetch(hist_ref.at[l, :, pl.ds(ROWS_A, ROWS_B)], kvb.at[l, zh, x, y]))
    second = [fetch(wout_ref.at[l], wout.at[l, c]) for l in range(2)]
    third = [fetch(win_ref.at[l], win.at[l]) for l in range(2)]

    barrier = pltpu.get_barrier_semaphore()
    friends = [right, left, up, down, over, ring_up, ring_down]
    friends += [(u, (c + k) % NC) for k in range(1, NC)]
    for friend in friends:
        pl.semaphore_signal(barrier, inc=1, device_id=friend, device_id_type=pl.DeviceIdType.MESH)
    pl.semaphore_wait(barrier, len(friends))

    sent = []

    def send(src, dst, to):
        n = len(sent)
        copy = pltpu.make_async_remote_copy(
            src_ref=src, dst_ref=dst, send_sem=send_sem.at[n], recv_sem=recv_sem.at[n],
            device_id=to, device_id_type=pl.DeviceIdType.MESH,
        )
        copy.start()
        sent.append(copy)
        return copy

    def same(ref, to):
        return send(ref, ref, to)

    def got(copies):
        for copy in copies:
            copy.wait_recv()

    class Chain:
        def __init__(self, l, z):
            self.l, self.z = l, z

        def a(self, yy, *rest):
            return kva.at[(self.l, self.z, yy) + rest]

        def b(self, xx, *rest):
            return kvb.at[(self.l, self.z, xx) + rest]

        def a0(self):
            s = self.a(y, x)
            self.ax = [same(s, right), same(s, left)]

        def a1(self):
            got(self.ax)
            self.ax = [same(self.a(y, xs[3], 0), right), same(self.a(y, xs[1], 1), left)]

        def a2(self):
            got(self.ax)
            s = self.a(y)
            self.ay = [same(s, up), same(s, down)]

        def a3(self):
            got(self.ay)
            self.ay = [same(self.a(ys[7]), up), same(self.a(ys[1]), down)]

        def a4(self):
            got(self.ay)
            self.ay = [same(self.a(ys[6]), up), same(self.a(ys[2]), down)]

        def a5(self):
            got(self.ay)
            self.ay = [
                same(self.a(ys[5], pl.ds(0, 2)), up),
                same(self.a(ys[3], pl.ds(2, 2)), down),
            ]

        def a6(self):
            got(self.ay)

        def row(self, *at_y):
            for yy in at_y:
                s = self.b(x, yy)
                self.bx += [same(s, right), same(s, left)]

        def b0(self):
            s = self.b(x, y)
            self.by, self.bx = [same(s, up), same(s, down)], []
            self.row(y)

        def b1(self):
            got(self.by)
            self.by = [same(self.b(x, ys[7]), up), same(self.b(x, ys[1]), down)]
            self.row(ys[7], ys[1])

        def b2(self):
            got(self.by)
            self.by = [same(self.b(x, ys[6]), up), same(self.b(x, ys[2]), down)]
            self.row(ys[6], ys[2])

        def b3(self):
            got(self.by)
            self.by = [same(self.b(x, ys[5], 0), up), same(self.b(x, ys[3], 1), down)]
            self.row(ys[5], ys[3])

        def b4(self):
            got(self.by)
            self.row(ys[4])

        def b5(self):
            got(self.bx)
            self.bx = [
                same(self.b(xs[3], pl.ds(0, 4)), right),
                same(self.b(xs[1], pl.ds(4, 4)), left),
            ]

        def b6(self):
            got(self.bx)

    def scores(k, m, v):
        s = lax.dot_general(
            qp[...], jnp.concatenate([k, m], axis=1), (((1,), (1,)), ((), ())),
            preferred_element_type=jnp.float32,
        )
        w = half_silu(s.astype(jnp.bfloat16))
        acc[...] += jnp.dot(w, v, preferred_element_type=jnp.float32)

    def attend_a(l, low, number):
        @pl.loop(low, low + number)
        def _(i):
            n = NZ * NX * ROWS_A

            def both(ref, *rest):
                return jnp.concatenate([
                    ref[(slice(None), yy, slice(None)) + rest].reshape(n, DH)
                    for yy in ((y + NY - i) % NY, (y + 1 + i) % NY)
                ])

            scores(both(kva.at[l], 0), both(ma), both(kva.at[l], 1))

    def attend_b(l, low, number):
        @pl.loop(low, low + number)
        def _(i):
            xx = (x + i) % NX
            n = NZ * NY * ROWS_B
            scores(
                kvb[l, :, xx, :, 0].reshape(n, DH),
                mb[:, xx].reshape(n, DH),
                kvb[l, :, xx, :, 1].reshape(n, DH),
            )

    def project(l, rows, value):
        mixed = jnp.dot(value, win[l], preferred_element_type=jnp.float32)
        p = half_silu(0.5 * mixed)
        q = (p[:, 2 * DH:3 * DH] * (0.5 * SCALE)).astype(jnp.bfloat16)
        p = p.astype(jnp.bfloat16)
        gate[rows, :] = p[:, :DH]
        qp[rows, pl.ds(0, DH)] = q
        own = jnp.sum(
            q.astype(jnp.float32) * p[:, 3 * DH:].astype(jnp.float32), axis=1, keepdims=True
        )
        own = half_silu(own).astype(jnp.bfloat16).astype(jnp.float32)
        acc[rows, :] = own * p[:, DH:2 * DH].astype(jnp.float32)

    def gated(rows):
        a = acc[rows, :]
        centred = a - jnp.mean(a, axis=1, keepdims=True)
        variance = jnp.mean(centred * centred, axis=1, keepdims=True)
        return (
            centred * lax.rsqrt(variance + 1e-05) * gate[rows, :].astype(jnp.float32)
        ).astype(jnp.bfloat16)

    class Weights:
        def __init__(self, l):
            self.l = l

        def slot(self, k):
            return zls[k % 4] * 2 + core

        def w1(self):
            s = wout.at[self.l, c]
            self.z = [same(s, ring_up), same(s, ring_down)]
            self.s = [same(s, (u, sib))]

        def w2(self):
            got(self.z)
            below, above = wout.at[self.l, self.slot(3)], wout.at[self.l, self.slot(1)]
            self.z = [
                same(below.at[pl.ds(0, 64)], ring_up), same(above.at[pl.ds(64, 64)], ring_down)
            ]
            self.s += [same(below, (u, sib)), same(above, (u, sib))]

        def w3(self):
            got(self.z)
            self.s += [same(wout.at[self.l, self.slot(2)], (u, sib))]

        def w4(self):
            got(self.s)

    for copy in first:
        copy.wait()
    def cross(l):
        return [same(kva.at[l, zh, y, x], over), same(kvb.at[l, zh, x, y], over)]

    across = [cross(0)]
    (o, p), (o1, p1) = [[Chain(l, zh), Chain(l, 1 - zh)] for l in range(2)]
    o.b0()
    o.a0()
    xsend = [same(xg.at[c], line(k)) for k in range(1, 4)]
    xshare = [same(xg.at[c], (u, sib))]
    w0, w1 = Weights(0), Weights(1)

    lane = lax.broadcasted_iota(jnp.int32, (BLOCK, BLOCK), 1)
    sub = lax.broadcasted_iota(jnp.int32, (BLOCK, BLOCK), 0)

    @pl.loop(0, NX * NY * NZ)
    def _(b):
        by, bz, bx = b // 8, (b // 4) % 2, b % 4
        owner = user_ref[b]
        valid = length_ref[owner] - place_ref[b] * BLOCK
        code = jnp.where(sub < valid, owner, USERS)
        hot = jnp.where(lane == code, 1.0, 0.0).astype(jnp.bfloat16)
        ma[bz, by, bx] = hot[:ROWS_A]
        mb[bz, bx, by] = hot[ROWS_A:]

    @pl.loop(0, GROUP // BLOCK)
    def _(t):
        row = u * GROUP + t * BLOCK + sub
        end = count_ref[0]
        cu = (row >= end).astype(jnp.int32)
        for k in range(1, USERS):
            end = end + count_ref[k]
            cu = cu + (row >= end).astype(jnp.int32)
        hide = jnp.where((lane == cu) | (lane > USERS), 0.0, HIDE)
        qp[pl.ds(pl.multiple_of(t * BLOCK, BLOCK), BLOCK), pl.ds(DH, DH)] = hide.astype(jnp.bfloat16)

    o.b1()
    o.a1()
    o.b2()
    got(across[0])
    p.b0()
    p.a0()
    o.a2()
    o.b3()
    p.b1()
    p.a1()
    o.a3()
    o.b4()
    p.b2()
    p.a2()
    o.a4()
    o.b5()
    for k in range(1, 4):
        got([xsend[k - 1]])
        xshare.append(same(xg.at[zls[4 - k] * 2 + core], (u, sib)))
    across.append(cross(1))
    for copy in second:
        copy.wait()
    w0.w1()
    p.b3()
    for copy in third:
        copy.wait()
    got(xshare)

    @pl.loop(0, 4)
    def _(t):
        part = pl.ds(pl.multiple_of(t * 2, 2), 2)
        rows = pl.ds(pl.multiple_of(t * BLOCK, BLOCK), BLOCK)
        project(0, rows, xg[part].reshape(BLOCK, D))

    p.a3()
    attend_a(0, 0, 1)
    o.a5()
    o.b6()
    p.b4()
    attend_b(0, 0, 1)
    o1.b0()
    got(across[1])
    p1.b0()
    o1.a0()
    p1.a0()
    w0.w2()
    p.a4()
    attend_a(0, 1, 1)
    p.b5()
    attend_b(0, 1, 1)
    o.a6()
    attend_b(0, 3, 1)
    o1.b1()
    o1.a1()
    p1.b1()
    p1.a1()
    p.a5()
    w0.w3()
    attend_a(0, 2, 1)
    o1.b2()
    p.b6()
    p1.b2()
    attend_b(0, 2, 1)
    p.a6()
    attend_a(0, 3, 1)
    o1.b3()
    o1.a2()
    size = GROUP // CHUNKS
    gsend, gshare = [], []
    for r in range(CHUNKS):
        rows = pl.ds(r * size, size)
        gat[c, rows] = gated(rows)
        gsend.append([same(gat.at[c, rows], line(k)) for k in range(1, 4)])
        gshare.append([same(gat.at[c, rows], (u, sib))])
    def pass_on(r):
        rows = pl.ds(r * size, size)
        for k in range(1, 4):
            got([gsend[r][k - 1]])
            gshare[r].append(same(gat.at[zls[4 - k] * 2 + core, rows], (u, sib)))

    def next_layer(r):
        got(gshare[r])

        @pl.loop(0, size // BLOCK)
        def _(t):
            first_row = r * size + t * BLOCK
            rows = pl.ds(pl.multiple_of(first_row, BLOCK), BLOCK)
            part = pl.ds(pl.multiple_of(r * (size // OWN) + t * 2, 2), 2)
            g = jnp.concatenate([gat[h, rows] for h in range(NC)], axis=1)
            term = jnp.dot(g, wout[0].reshape(D, D), preferred_element_type=jnp.float32)
            new = (xg[part].reshape(BLOCK, D).astype(jnp.float32) + term).astype(jnp.bfloat16)
            x1[rows, :] = new
            project(1, rows, new)

    p1.b3()
    p1.a2()
    o1.b4()
    o1.a3()
    p1.b4()
    pass_on(0)
    w0.w4()
    next_layer(0)
    p1.a3()
    o1.a4()
    pass_on(1)
    w1.w1()
    o1.b5()
    p1.b5()
    next_layer(1)
    p1.a4()
    attend_a(1, 0, 1)
    attend_a(1, 1, 1)
    o1.a5()
    attend_b(1, 0, 1)
    o1.b6()
    w1.w2()
    attend_b(1, 1, 1)
    attend_b(1, 3, 1)
    p1.a5()
    attend_a(1, 2, 1)
    o1.a6()
    p1.b6()
    attend_b(1, 2, 1)
    p1.a6()
    attend_a(1, 3, 1)
    gown[...] = gated(slice(None))
    back = []
    for k in range(1, NC):
        to = (c + k) % NC
        rows = pl.ds(pl.multiple_of(to * OWN, OWN), OWN)
        back.append(send(gown.at[rows], g1.at[c], (u, to)))
    w1.w3()
    mine = pl.ds(pl.multiple_of(c * OWN, OWN), OWN)
    g1[c] = gown[mine, :]
    got(back)
    w1.w4()
    g = jnp.concatenate([g1[h] for h in range(NC)], axis=1)
    term = jnp.dot(g, wout[1].reshape(D, D), preferred_element_type=jnp.float32)
    out_ref[...] = (x1[mine, :].astype(jnp.float32) + term).astype(jnp.bfloat16)
    for copy in sent:
        copy.wait_send()


def body(rows, weight_in, weight_out, cache, block_user, block_offset, length, count):
    bf16 = jnp.bfloat16
    hbm, smem = pl.BlockSpec(memory_space=pl.ANY), pl.BlockSpec(memory_space=pltpu.SMEM)
    return pl.pallas_call(
        kernel,
        out_shape=jax.ShapeDtypeStruct((OWN, D), bf16),
        in_specs=[hbm] * 4 + [smem] * 4,
        out_specs=pl.BlockSpec(memory_space=pltpu.VMEM),
        scratch_shapes=[
            pltpu.VMEM((2, NZ, NY, NX, 2, ROWS_A, DH), bf16),
            pltpu.VMEM((2, NZ, NX, NY, 2, ROWS_B, DH), bf16),
            pltpu.VMEM((NZ, NY, NX, ROWS_A, DH), bf16),
            pltpu.VMEM((NZ, NX, NY, ROWS_B, DH), bf16),
            pltpu.VMEM((NC, OWN, D), bf16),
            pltpu.VMEM((GROUP, D), bf16),
            pltpu.VMEM((2, D, 4 * DH), bf16),
            pltpu.VMEM((2, NC, DH, D), bf16),
            pltpu.VMEM((GROUP, 2 * DH), bf16),
            pltpu.VMEM((GROUP, DH), bf16),
            pltpu.VMEM((GROUP, DH), jnp.float32),
            pltpu.VMEM((NC, GROUP, DH), bf16),
            pltpu.VMEM((GROUP, DH), bf16),
            pltpu.VMEM((NC, OWN, DH), bf16),
            pltpu.SemaphoreType.DMA((MESSAGES,)),
            pltpu.SemaphoreType.DMA((MESSAGES,)),
            pltpu.SemaphoreType.DMA((9,)),
        ],
        compiler_params=pltpu.CompilerParams(
            collective_id=0, has_side_effects=True, vmem_limit_bytes=60 * 1024 * 1024
        ),
        cost_estimate=pl.CostEstimate(
            flops=12_000_000_000, bytes_accessed=4_000_000, transcendentals=9_000_000
        ),
    )(
        rows,
        weight_in.reshape(2, D, 4 * DH),
        weight_out.reshape(2, DH, D),
        cache.reshape(2, 2, BLOCK, DH),
        block_user,
        block_offset,
        length,
        count,
    )


def solution(mesh):
    placed = (
        P(("users", "cand"), None),
        P(None, None, "cand", None),
        P(None, "cand", None, None),
        P(None, None, "users", "cand", None),
        P(),
        P(),
        P(),
        P(),
    )
    return jax.shard_map(
        body, mesh=mesh, in_specs=placed, out_specs=P(("users", "cand"), None), check_vma=False
    )
```

```python
import math

import jax
import jax.numpy as jnp
from jax import lax
from jax.experimental import pallas as pl
from jax.experimental.pallas import tpu as pltpu
from jax.sharding import PartitionSpec as P

BLOCK = 128
NX, NY, NZ, NC = 4, 8, 2, 8
ROWS_A, ROWS_B = 48, 80
OWN, D, DH, USERS = 64, 1024, 128, 16
GROUP = OWN * NC
HIDE = -1e30
CHUNKS = 2
ARRIVALS, DEPARTURES = 80, 11
SCALE = 1.0 / math.sqrt(DH)


def half_silu(h):
    return h * jnp.tanh(h) + h


def kernel(
    x_ref, win_ref, wout_ref, hist_ref, user_in, place_in, length_in, count_in, out_ref,
    kva, kvb, ma, mb, xg, x1, win, wout, qp, gate, acc, gat, gown, g1,
    user_ref, place_ref, length_ref, count_ref, send_sem, recv_sem, local_sem,
):
    u, c = lax.axis_index("users"), lax.axis_index("cand")
    y, zh, x = u // 8, (u // 4) % 2, u % 4
    zl, core = c // 2, c % 2
    sib = zl * 2 + (1 - core)

    def at(y_, zh_, x_):
        return y_ * 8 + zh_ * 4 + x_

    xs = [(x + k) % NX for k in range(NX)]
    ys = [(y + k) % NY for k in range(NY)]
    right, left = (at(y, zh, xs[1]), c), (at(y, zh, xs[3]), c)
    up, down = (at(ys[1], zh, x), c), (at(ys[7], zh, x), c)
    over = (at(y, 1 - zh, x), c)
    z8 = zh * 4 + zl
    zu, zd = (z8 + 1) % 8, (z8 + 7) % 8
    ring_up = (at(y, zu // 4, x), (zu % 4) * 2 + core)
    ring_down = (at(y, zd // 4, x), (zd % 4) * 2 + core)
    zls = [(zl + k) % 4 for k in range(4)]

    def line(k):
        return (u, zls[k] * 2 + core)

    local = []

    def fetch(src, dst):
        copy = pltpu.make_async_copy(src, dst, local_sem.at[len(local)])
        copy.start()
        local.append(copy)
        return copy

    first = [fetch(x_ref, xg.at[c])]
    for l in range(2):
        first.append(fetch(hist_ref.at[l, :, pl.ds(0, ROWS_A)], kva.at[l, zh, y, x]))
        first.append(fetch(hist_ref.at[l, :, pl.ds(ROWS_A, ROWS_B)], kvb.at[l, zh, x, y]))
    small = [
        fetch(src, dst)
        for src, dst in (
            (user_in, user_ref), (place_in, place_ref), (length_in, length_ref), (count_in, count_ref)
        )
    ]
    second = [fetch(wout_ref.at[l], wout.at[l, c]) for l in range(2)]
    third = [fetch(win_ref.at[l], win.at[l]) for l in range(2)]

    barrier = pltpu.get_barrier_semaphore()
    friends = [right, left, up, down, over, ring_up, ring_down]
    friends += [(u, (c + k) % NC) for k in range(1, NC)]
    for friend in friends:
        pl.semaphore_signal(barrier, inc=1, device_id=friend, device_id_type=pl.DeviceIdType.MESH)
    pl.semaphore_wait(barrier, len(friends))

    AY, AX, BY, BH, BX, CA, CB, XS, WS, GS, HS = range(DEPARTURES)
    arrivals = []

    class Batch:
        def __init__(self, size):
            self.sem, self.size = recv_sem.at[len(arrivals)], size
            arrivals.append(self)

        def send(self, kind, src, dst, to):
            pltpu.make_async_remote_copy(
                src_ref=src, dst_ref=dst, send_sem=send_sem.at[kind], recv_sem=self.sem,
                device_id=to, device_id_type=pl.DeviceIdType.MESH,
            ).start()
            return self

        def same(self, kind, *pairs):
            for ref, to in pairs:
                self.send(kind, ref, ref, to)
            return self

        def got(self):
            pltpu.make_async_copy(self.size, self.size, self.sem).wait()

    class Chain:
        def __init__(self, l, z):
            self.l, self.z = l, z

        def a(self, yy, *rest):
            return kva.at[(self.l, self.z, yy) + rest]

        def b(self, xx, *rest):
            return kvb.at[(self.l, self.z, xx) + rest]

        def a0(self):
            s = self.a(y, x)
            self.ax = Batch(kva.at[0, 0, 0, pl.ds(0, 2)]).same(AX, (s, right), (s, left))

        def a1(self):
            self.ax.got()
            self.ax = Batch(kva.at[0, 0, 0, 0]).same(
                AX, (self.a(y, xs[3], 0), right), (self.a(y, xs[1], 1), left)
            )

        def go_y(self, one, other):
            self.ay = Batch(kva.at[0, 0, pl.ds(0, 2)]).same(
                AY, (self.a(one), up), (self.a(other), down)
            )

        def a2(self):
            self.ax.got()
            self.go_y(y, y)

        def a3(self):
            self.ay.got()
            self.go_y(ys[7], ys[1])

        def a4(self):
            self.ay.got()
            self.go_y(ys[6], ys[2])

        def a5(self):
            self.ay.got()
            self.ay = Batch(kva.at[0, 0, 0]).same(
                AX, (self.a(ys[5], pl.ds(0, 2)), up), (self.a(ys[3], pl.ds(2, 2)), down)
            )

        def a6(self):
            self.ay.got()

        def row(self, *at_y):
            for yy in at_y:
                s = self.b(x, yy)
                self.bx.same(BX, (s, right), (s, left))

        def go_b(self, one, other):
            self.by = Batch(kvb.at[0, 0, 0, pl.ds(0, 2)]).same(
                BY, (self.b(x, one), up), (self.b(x, other), down)
            )

        def b0(self):
            self.bx = Batch(kvb.at[0, 0, pl.ds(0, 2)])
            self.go_b(y, y)
            self.row(y)

        def b1(self):
            self.by.got()
            self.go_b(ys[7], ys[1])
            self.row(ys[7], ys[1])

        def b2(self):
            self.by.got()
            self.go_b(ys[6], ys[2])
            self.row(ys[6], ys[2])

        def b3(self):
            self.by.got()
            self.by = Batch(kvb.at[0, 0, 0, 0]).same(
                BH, (self.b(x, ys[5], 0), up), (self.b(x, ys[3], 1), down)
            )
            self.row(ys[5], ys[3])

        def b4(self):
            self.by.got()
            self.row(ys[4])

        def b5(self):
            self.bx.got()
            self.bx = Batch(kvb.at[0, 0, 0]).same(
                BX, (self.b(xs[3], pl.ds(0, 4)), right), (self.b(xs[1], pl.ds(4, 4)), left)
            )

        def b6(self):
            self.bx.got()

    def scores(k, m, v):
        s = lax.dot_general(
            qp[...], jnp.concatenate([k, m], axis=1), (((1,), (1,)), ((), ())),
            preferred_element_type=jnp.float32,
        )
        w = half_silu(s.astype(jnp.bfloat16))
        acc[...] += jnp.dot(w, v, preferred_element_type=jnp.float32)

    def attend_a(l, low, number):
        @pl.loop(low, low + number)
        def _(i):
            n = NZ * NX * ROWS_A

            def both(ref, *rest):
                return jnp.concatenate([
                    ref[(slice(None), yy, slice(None)) + rest].reshape(n, DH)
                    for yy in ((y + NY - i) % NY, (y + 1 + i) % NY)
                ])

            scores(both(kva.at[l], 0), both(ma), both(kva.at[l], 1))

    def attend_b(l, low, number):
        @pl.loop(low, low + number)
        def _(i):
            xx = (x + i) % NX
            n = NZ * NY * ROWS_B
            scores(
                kvb[l, :, xx, :, 0].reshape(n, DH),
                mb[:, xx].reshape(n, DH),
                kvb[l, :, xx, :, 1].reshape(n, DH),
            )

    def project(l, rows, value):
        mixed = jnp.dot(value, win[l], preferred_element_type=jnp.float32)
        p = half_silu(0.5 * mixed)
        q = (p[:, 2 * DH:3 * DH] * (0.5 * SCALE)).astype(jnp.bfloat16)
        p = p.astype(jnp.bfloat16)
        gate[rows, :] = p[:, :DH]
        qp[rows, pl.ds(0, DH)] = q
        own = jnp.sum(
            q.astype(jnp.float32) * p[:, 3 * DH:].astype(jnp.float32), axis=1, keepdims=True
        )
        own = half_silu(own).astype(jnp.bfloat16).astype(jnp.float32)
        acc[rows, :] = own * p[:, DH:2 * DH].astype(jnp.float32)

    def gated(rows):
        a = acc[rows, :]
        centred = a - jnp.mean(a, axis=1, keepdims=True)
        variance = jnp.mean(centred * centred, axis=1, keepdims=True)
        return (
            centred * lax.rsqrt(variance + 1e-05) * gate[rows, :].astype(jnp.float32)
        ).astype(jnp.bfloat16)

    class Weights:
        def __init__(self, l):
            self.l = l

        def slot(self, k):
            return zls[k % 4] * 2 + core

        def w1(self):
            s = wout.at[self.l, c]
            self.z = Batch(wout.at[0, pl.ds(0, 2)]).same(WS, (s, ring_up), (s, ring_down))
            self.s = Batch(wout.at[0, pl.ds(0, 4)]).same(WS, (s, (u, sib)))

        def w2(self):
            self.z.got()
            below, above = wout.at[self.l, self.slot(3)], wout.at[self.l, self.slot(1)]
            self.z = Batch(wout.at[0, 0]).same(
                WS, (below.at[pl.ds(0, 64)], ring_up), (above.at[pl.ds(64, 64)], ring_down)
            )
            self.s.same(WS, (below, (u, sib)), (above, (u, sib)))

        def w3(self):
            self.z.got()
            self.s.same(WS, (wout.at[self.l, self.slot(2)], (u, sib)))

        def w4(self):
            self.s.got()

    for copy in first:
        copy.wait()
    def cross(l):
        return [
            Batch(kva.at[0, 0, 0, 0]).same(CA, (kva.at[l, zh, y, x], over)),
            Batch(kvb.at[0, 0, 0, 0]).same(CB, (kvb.at[l, zh, x, y], over)),
        ]

    def crossed(l):
        for batch in across[l]:
            batch.got()

    across = [cross(0)]
    (o, p), (o1, p1) = [[Chain(l, zh), Chain(l, 1 - zh)] for l in range(2)]
    o.b0()
    o.a0()
    w0, w1 = Weights(0), Weights(1)

    lane = lax.broadcasted_iota(jnp.int32, (BLOCK, BLOCK), 1)
    sub = lax.broadcasted_iota(jnp.int32, (BLOCK, BLOCK), 0)

    xsend = [Batch(xg.at[0]).same(XS, (xg.at[c], line(k))) for k in range(1, 4)]
    xshare = Batch(xg.at[pl.ds(0, 4)]).same(XS, (xg.at[c], (u, sib)))
    for copy in small:
        copy.wait()

    @pl.loop(0, NX * NY * NZ)
    def _(b):
        by, bz, bx = b // 8, (b // 4) % 2, b % 4
        owner = user_ref[b]
        valid = length_ref[owner] - place_ref[b] * BLOCK
        code = jnp.where(sub < valid, owner, USERS)
        hot = jnp.where(lane == code, 1.0, 0.0).astype(jnp.bfloat16)
        ma[bz, by, bx] = hot[:ROWS_A]
        mb[bz, bx, by] = hot[ROWS_A:]

    @pl.loop(0, GROUP // BLOCK)
    def _(t):
        row = u * GROUP + t * BLOCK + sub
        end = count_ref[0]
        cu = (row >= end).astype(jnp.int32)
        for k in range(1, USERS):
            end = end + count_ref[k]
            cu = cu + (row >= end).astype(jnp.int32)
        hide = jnp.where((lane == cu) | (lane > USERS), 0.0, HIDE)
        qp[pl.ds(pl.multiple_of(t * BLOCK, BLOCK), BLOCK), pl.ds(DH, DH)] = hide.astype(jnp.bfloat16)

    o.b1()
    o.a1()
    o.b2()
    crossed(0)
    p.b0()
    p.a0()
    o.a2()
    p.b1()
    p.a1()
    o.b3()
    o.a3()
    p.b2()
    o.b4()
    p.a2()
    for k in range(1, 4):
        xsend[k - 1].got()
        xshare.same(XS, (xg.at[zls[4 - k] * 2 + core], (u, sib)))
    across.append(cross(1))
    for copy in second:
        copy.wait()
    w0.w1()
    for copy in third:
        copy.wait()
    xshare.got()

    @pl.loop(0, 4)
    def _(t):
        part = pl.ds(pl.multiple_of(t * 2, 2), 2)
        rows = pl.ds(pl.multiple_of(t * BLOCK, BLOCK), BLOCK)
        project(0, rows, xg[part].reshape(BLOCK, D))

    p.b3()
    o.a4()
    o.b5()
    p.a3()
    attend_a(0, 0, 1)
    p.b4()
    attend_b(0, 0, 1)
    o1.b0()
    crossed(1)
    p1.b0()
    o1.a0()
    p1.a0()
    w0.w2()
    o.a5()
    p.a4()
    attend_a(0, 1, 1)
    o.b6()
    o1.b1()
    p.b5()
    attend_b(0, 1, 1)
    p1.b1()
    w0.w3()
    w1.w1()
    attend_b(0, 3, 1)
    o.a6()
    o1.a1()
    p1.a1()
    p.a5()
    attend_a(0, 2, 1)
    o1.b2()
    p1.b2()
    p.a6()
    attend_a(0, 3, 1)
    o1.b3()
    p1.b3()
    p.b6()
    attend_b(0, 2, 1)
    size = GROUP // CHUNKS
    halves = [pl.ds(r * size, size) for r in range(CHUNKS)]
    gsend, gshare = [], []

    def spread(r):
        own = gat.at[c, halves[r]]
        one = gat.at[0, pl.ds(0, size)]
        gsend.append([Batch(one).same(GS, (own, line(k))) for k in range(1, 4)])
        gshare.append(
            Batch(gat.at[pl.ds(0, 4), pl.ds(0, size)]).same(GS, (own, (u, sib)))
        )

    gat[c, halves[0]] = gated(halves[0])
    spread(0)
    gat[c, halves[1]] = gated(halves[1])

    def pass_on(r):
        for k in range(1, 4):
            gsend[r][k - 1].got()
            gshare[r].same(GS, (gat.at[zls[4 - k] * 2 + core, halves[r]], (u, sib)))

    def next_layer(r):
        gshare[r].got()

        @pl.loop(0, size // BLOCK)
        def _(t):
            first_row = r * size + t * BLOCK
            rows = pl.ds(pl.multiple_of(first_row, BLOCK), BLOCK)
            part = pl.ds(pl.multiple_of(r * (size // OWN) + t * 2, 2), 2)
            g = jnp.concatenate([gat[h, rows] for h in range(NC)], axis=1)
            term = jnp.dot(g, wout[0].reshape(D, D), preferred_element_type=jnp.float32)
            new = (xg[part].reshape(BLOCK, D).astype(jnp.float32) + term).astype(jnp.bfloat16)
            x1[rows, :] = new
            project(1, rows, new)

    o1.b4()
    o1.a2()
    p1.b4()
    p1.a2()
    o1.a3()
    pass_on(0)
    spread(1)
    p1.a3()
    w0.w4()
    next_layer(0)
    o1.a4()
    o1.b5()
    p1.a4()
    pass_on(1)
    p1.b5()
    next_layer(1)
    w1.w2()
    attend_a(1, 0, 1)
    attend_a(1, 1, 1)
    o1.a5()
    o1.b6()
    attend_b(1, 0, 1)
    attend_b(1, 1, 1)
    attend_b(1, 3, 1)
    w1.w3()
    p1.a5()
    attend_a(1, 2, 1)
    o1.a6()
    p1.b6()
    attend_b(1, 2, 1)
    p1.a6()
    attend_a(1, 3, 1)
    gown[...] = gated(slice(None))
    back = Batch(g1.at[pl.ds(0, NC - 1)])
    for k in range(1, NC):
        to = (c + k) % NC
        rows = pl.ds(pl.multiple_of(to * OWN, OWN), OWN)
        back.send(HS, gown.at[rows], g1.at[c], (u, to))
    mine = pl.ds(pl.multiple_of(c * OWN, OWN), OWN)
    g1[c] = gown[mine, :]
    back.got()
    w1.w4()
    g = jnp.concatenate([g1[h] for h in range(NC)], axis=1)
    term = jnp.dot(g, wout[1].reshape(D, D), preferred_element_type=jnp.float32)
    out_ref[...] = (x1[mine, :].astype(jnp.float32) + term).astype(jnp.bfloat16)
    everything = {
        AY: kva.at[:, :, pl.ds(0, 6)],
        AX: kva.at[0, 0, pl.ds(0, 7)],
        BY: kvb.at[0, 0, pl.ds(0, 3)],
        BH: kvb.at[0, 0, 0, pl.ds(0, 4)],
        BX: kvb.at[:, :, pl.ds(0, 3)],
        CA: kva.at[0, 0, 0, pl.ds(0, 2)],
        CB: kvb.at[0, 0, 0, pl.ds(0, 2)],
        XS: xg.at[pl.ds(0, 7)],
        WS: wout.at[:, pl.ds(0, 7)],
        GS: gat.at[pl.ds(0, 7)],
        HS: g1.at[pl.ds(0, 7)],
    }
    for kind, size_ref in everything.items():
        pltpu.make_async_copy(size_ref, size_ref, send_sem.at[kind]).wait()


def body(rows, weight_in, weight_out, cache, block_user, block_offset, length, count):
    bf16 = jnp.bfloat16
    hbm = pl.BlockSpec(memory_space=pl.ANY)
    return pl.pallas_call(
        kernel,
        out_shape=jax.ShapeDtypeStruct((OWN, D), bf16),
        in_specs=[hbm] * 8,
        out_specs=pl.BlockSpec(memory_space=pltpu.VMEM),
        scratch_shapes=[
            pltpu.VMEM((2, NZ, NY, NX, 2, ROWS_A, DH), bf16),
            pltpu.VMEM((2, NZ, NX, NY, 2, ROWS_B, DH), bf16),
            pltpu.VMEM((NZ, NY, NX, ROWS_A, DH), bf16),
            pltpu.VMEM((NZ, NX, NY, ROWS_B, DH), bf16),
            pltpu.VMEM((NC, OWN, D), bf16),
            pltpu.VMEM((GROUP, D), bf16),
            pltpu.VMEM((2, D, 4 * DH), bf16),
            pltpu.VMEM((2, NC, DH, D), bf16),
            pltpu.VMEM((GROUP, 2 * DH), bf16),
            pltpu.VMEM((GROUP, DH), bf16),
            pltpu.VMEM((GROUP, DH), jnp.float32),
            pltpu.VMEM((NC, GROUP, DH), bf16),
            pltpu.VMEM((GROUP, DH), bf16),
            pltpu.VMEM((NC, OWN, DH), bf16),
            pltpu.SMEM((64,), jnp.int32),
            pltpu.SMEM((64,), jnp.int32),
            pltpu.SMEM((16,), jnp.int32),
            pltpu.SMEM((16,), jnp.int32),
            pltpu.SemaphoreType.DMA((DEPARTURES,)),
            pltpu.SemaphoreType.DMA((ARRIVALS,)),
            pltpu.SemaphoreType.DMA((13,)),
        ],
        compiler_params=pltpu.CompilerParams(
            collective_id=0, has_side_effects=True, vmem_limit_bytes=60 * 1024 * 1024
        ),
        cost_estimate=pl.CostEstimate(
            flops=12_000_000_000, bytes_accessed=4_000_000, transcendentals=9_000_000
        ),
    )(
        rows,
        weight_in.reshape(2, D, 4 * DH),
        weight_out.reshape(2, DH, D),
        cache.reshape(2, 2, BLOCK, DH),
        block_user,
        block_offset,
        length,
        count,
    )


def solution(mesh):
    placed = (
        P(("users", "cand"), None),
        P(None, None, "cand", None),
        P(None, "cand", None, None),
        P(None, None, "users", "cand", None),
        P(),
        P(),
        P(),
        P(),
    )
    return jax.shard_map(
        body, mesh=mesh, in_specs=placed, out_specs=P(("users", "cand"), None), check_vma=False
    )
```

```python
import math

import jax
import jax.numpy as jnp
from jax import lax
from jax.experimental import pallas as pl
from jax.experimental.pallas import tpu as pltpu
from jax.sharding import PartitionSpec as P

BLOCK = 128
NX, NY, NZ, NC = 4, 8, 2, 8
ROWS_A, ROWS_B = 48, 80
OWN, D, DH, USERS = 64, 1024, 128, 16
GROUP = OWN * NC
HIDE = -1e30
CHUNKS = 2
ARRIVALS, DEPARTURES = 80, 11
SCALE = 1.0 / math.sqrt(DH)


def half_silu(h):
    return h * jnp.tanh(h) + h


def kernel(
    x_ref, win_ref, wout_ref, hist_ref, user_in, place_in, length_in, count_in, out_ref,
    kva, kvb, ma, mb, xg, x1, win, wout, qp, gate, acc, gat, gown, g1,
    user_ref, place_ref, length_ref, count_ref, send_sem, recv_sem, local_sem,
):
    u, c = lax.axis_index("users"), lax.axis_index("cand")
    y, zh, x = u // 8, (u // 4) % 2, u % 4
    zl, core = c // 2, c % 2
    sib = zl * 2 + (1 - core)

    def at(y_, zh_, x_):
        return y_ * 8 + zh_ * 4 + x_

    xs = [(x + k) % NX for k in range(NX)]
    ys = [(y + k) % NY for k in range(NY)]
    right, left = (at(y, zh, xs[1]), c), (at(y, zh, xs[3]), c)
    up, down = (at(ys[1], zh, x), c), (at(ys[7], zh, x), c)
    over = (at(y, 1 - zh, x), c)
    z8 = zh * 4 + zl
    zu, zd = (z8 + 1) % 8, (z8 + 7) % 8
    ring_up = (at(y, zu // 4, x), (zu % 4) * 2 + core)
    ring_down = (at(y, zd // 4, x), (zd % 4) * 2 + core)
    zls = [(zl + k) % 4 for k in range(4)]

    def line(k):
        return (u, zls[k] * 2 + core)

    local = []

    def fetch(src, dst):
        copy = pltpu.make_async_copy(src, dst, local_sem.at[len(local)])
        copy.start()
        local.append(copy)
        return copy

    first = [fetch(x_ref, xg.at[c])]
    for l in range(2):
        first.append(fetch(hist_ref.at[l, :, pl.ds(0, ROWS_A)], kva.at[l, zh, y, x]))
        first.append(fetch(hist_ref.at[l, :, pl.ds(ROWS_A, ROWS_B)], kvb.at[l, zh, x, y]))
    small = [
        fetch(src, dst)
        for src, dst in (
            (user_in, user_ref), (place_in, place_ref), (length_in, length_ref), (count_in, count_ref)
        )
    ]
    second = [fetch(wout_ref.at[l], wout.at[l, c]) for l in range(2)]
    third = [fetch(win_ref.at[l], win.at[l]) for l in range(2)]

    barrier = pltpu.get_barrier_semaphore()
    friends = [right, left, up, down, over, ring_up, ring_down]
    friends += [(u, (c + k) % NC) for k in range(1, NC)]
    for friend in friends:
        pl.semaphore_signal(barrier, inc=1, device_id=friend, device_id_type=pl.DeviceIdType.MESH)
    pl.semaphore_wait(barrier, len(friends))

    AY, AX, BY, BH, BX, CA, CB, XS, WS, GS, HS = range(DEPARTURES)
    arrivals = []

    class Batch:
        def __init__(self, size):
            self.sem, self.size = recv_sem.at[len(arrivals)], size
            arrivals.append(self)

        def send(self, kind, src, dst, to):
            pltpu.make_async_remote_copy(
                src_ref=src, dst_ref=dst, send_sem=send_sem.at[kind], recv_sem=self.sem,
                device_id=to, device_id_type=pl.DeviceIdType.MESH,
            ).start()
            return self

        def same(self, kind, *pairs):
            for ref, to in pairs:
                self.send(kind, ref, ref, to)
            return self

        def got(self):
            pltpu.make_async_copy(self.size, self.size, self.sem).wait()

    class Chain:
        def __init__(self, l, z):
            self.l, self.z = l, z

        def a(self, yy, *rest):
            return kva.at[(self.l, self.z, yy) + rest]

        def b(self, xx, *rest):
            return kvb.at[(self.l, self.z, xx) + rest]

        def a0(self):
            s = self.a(y, x)
            self.ax = Batch(kva.at[0, 0, 0, pl.ds(0, 2)]).same(AX, (s, right), (s, left))

        def a1(self):
            self.ax.got()
            self.ax = Batch(kva.at[0, 0, 0, 0]).same(
                AX, (self.a(y, xs[3], 0), right), (self.a(y, xs[1], 1), left)
            )

        def go_y(self, one, other):
            self.ay = Batch(kva.at[0, 0, pl.ds(0, 2)]).same(
                AY, (self.a(one), up), (self.a(other), down)
            )

        def a2(self):
            self.ax.got()
            self.go_y(y, y)

        def a3(self):
            self.ay.got()
            self.go_y(ys[7], ys[1])

        def a4(self):
            self.ay.got()
            self.go_y(ys[6], ys[2])

        def a5(self):
            self.ay.got()
            self.ay = Batch(kva.at[0, 0, 0]).same(
                AX, (self.a(ys[5], pl.ds(0, 2)), up), (self.a(ys[3], pl.ds(2, 2)), down)
            )

        def a6(self):
            self.ay.got()

        def row(self, *at_y):
            for yy in at_y:
                s = self.b(x, yy)
                self.bx.same(BX, (s, right), (s, left))

        def go_b(self, one, other):
            self.by = Batch(kvb.at[0, 0, 0, pl.ds(0, 2)]).same(
                BY, (self.b(x, one), up), (self.b(x, other), down)
            )

        def b0(self):
            self.bx = Batch(kvb.at[0, 0, pl.ds(0, 2)])
            self.go_b(y, y)
            self.row(y)

        def b1(self):
            self.by.got()
            self.go_b(ys[7], ys[1])
            self.row(ys[7], ys[1])

        def b2(self):
            self.by.got()
            self.go_b(ys[6], ys[2])
            self.row(ys[6], ys[2])

        def b3(self):
            self.by.got()
            self.by = Batch(kvb.at[0, 0, 0, 0]).same(
                BH, (self.b(x, ys[5], 0), up), (self.b(x, ys[3], 1), down)
            )
            self.row(ys[5], ys[3])

        def b4(self):
            self.by.got()
            self.row(ys[4])

        def b5(self):
            self.bx.got()
            self.bx = Batch(kvb.at[0, 0, 0]).same(
                BX, (self.b(xs[3], pl.ds(0, 4)), right), (self.b(xs[1], pl.ds(4, 4)), left)
            )

        def b6(self):
            self.bx.got()

    def scores(k, m, v):
        s = lax.dot_general(
            qp[...], jnp.concatenate([k, m], axis=1), (((1,), (1,)), ((), ())),
            preferred_element_type=jnp.float32,
        )
        w = half_silu(jnp.maximum(s, -100.0)).astype(jnp.bfloat16)
        acc[...] += jnp.dot(w, v, preferred_element_type=jnp.float32)

    def attend_a(l, low, number):
        @pl.loop(low, low + number)
        def _(i):
            n = NZ * NX * ROWS_A

            def both(ref, *rest):
                return jnp.concatenate([
                    ref[(slice(None), yy, slice(None)) + rest].reshape(n, DH)
                    for yy in ((y + NY - i) % NY, (y + 1 + i) % NY)
                ])

            scores(both(kva.at[l], 0), both(ma), both(kva.at[l], 1))

    def attend_b(l, low, number):
        @pl.loop(low, low + number)
        def _(i):
            xx = (x + i) % NX
            n = NZ * NY * ROWS_B
            scores(
                kvb[l, :, xx, :, 0].reshape(n, DH),
                mb[:, xx].reshape(n, DH),
                kvb[l, :, xx, :, 1].reshape(n, DH),
            )

    def project(l, rows, value):
        mixed = jnp.dot(value, win[l], preferred_element_type=jnp.float32)
        p = half_silu(0.5 * mixed)
        q = (p[:, 2 * DH:3 * DH] * (0.5 * SCALE)).astype(jnp.bfloat16)
        p = p.astype(jnp.bfloat16)
        gate[rows, :] = p[:, :DH]
        qp[rows, pl.ds(0, DH)] = q
        own = jnp.sum(
            q.astype(jnp.float32) * p[:, 3 * DH:].astype(jnp.float32), axis=1, keepdims=True
        )
        own = half_silu(own).astype(jnp.bfloat16).astype(jnp.float32)
        acc[rows, :] = own * p[:, DH:2 * DH].astype(jnp.float32)

    def gated(rows):
        a = acc[rows, :]
        centred = a - jnp.mean(a, axis=1, keepdims=True)
        variance = jnp.mean(centred * centred, axis=1, keepdims=True)
        return (
            centred * lax.rsqrt(variance + 1e-05) * gate[rows, :].astype(jnp.float32)
        ).astype(jnp.bfloat16)

    class Weights:
        def __init__(self, l):
            self.l = l

        def slot(self, k):
            return zls[k % 4] * 2 + core

        def w1(self):
            s = wout.at[self.l, c]
            self.z = Batch(wout.at[0, pl.ds(0, 2)]).same(WS, (s, ring_up), (s, ring_down))
            self.s = Batch(wout.at[0, pl.ds(0, 4)]).same(WS, (s, (u, sib)))

        def w2(self):
            self.z.got()
            below, above = wout.at[self.l, self.slot(3)], wout.at[self.l, self.slot(1)]
            self.z = Batch(wout.at[0, 0]).same(
                WS, (below.at[pl.ds(0, 64)], ring_up), (above.at[pl.ds(64, 64)], ring_down)
            )
            self.s.same(WS, (below, (u, sib)), (above, (u, sib)))

        def w3(self):
            self.z.got()
            self.s.same(WS, (wout.at[self.l, self.slot(2)], (u, sib)))

        def w4(self):
            self.s.got()

    for copy in first:
        copy.wait()
    def cross(l):
        return [
            Batch(kva.at[0, 0, 0, 0]).same(CA, (kva.at[l, zh, y, x], over)),
            Batch(kvb.at[0, 0, 0, 0]).same(CB, (kvb.at[l, zh, x, y], over)),
        ]

    def crossed(l):
        for batch in across[l]:
            batch.got()

    across = [cross(0)]
    (o, p), (o1, p1) = [[Chain(l, zh), Chain(l, 1 - zh)] for l in range(2)]
    o.b0()
    o.a0()
    w0, w1 = Weights(0), Weights(1)

    lane = lax.broadcasted_iota(jnp.int32, (BLOCK, BLOCK), 1)
    sub = lax.broadcasted_iota(jnp.int32, (BLOCK, BLOCK), 0)

    xsend = [Batch(xg.at[0]).same(XS, (xg.at[c], line(k))) for k in range(1, 4)]
    xshare = Batch(xg.at[pl.ds(0, 4)]).same(XS, (xg.at[c], (u, sib)))
    for copy in small:
        copy.wait()

    @pl.loop(0, NX * NY * NZ)
    def _(b):
        by, bz, bx = b // 8, (b // 4) % 2, b % 4
        owner = user_ref[b]
        valid = length_ref[owner] - place_ref[b] * BLOCK
        code = jnp.where(sub < valid, owner, USERS)
        hot = jnp.where(lane == code, 1.0, 0.0).astype(jnp.bfloat16)
        ma[bz, by, bx] = hot[:ROWS_A]
        mb[bz, bx, by] = hot[ROWS_A:]

    @pl.loop(0, GROUP // BLOCK)
    def _(t):
        row = u * GROUP + t * BLOCK + sub
        end = count_ref[0]
        cu = (row >= end).astype(jnp.int32)
        for k in range(1, USERS):
            end = end + count_ref[k]
            cu = cu + (row >= end).astype(jnp.int32)
        hide = jnp.where((lane == cu) | (lane > USERS), 0.0, HIDE)
        qp[pl.ds(pl.multiple_of(t * BLOCK, BLOCK), BLOCK), pl.ds(DH, DH)] = hide.astype(jnp.bfloat16)

    o.b1()
    o.a1()
    o.b2()
    crossed(0)
    p.b0()
    p.a0()
    o.a2()
    p.b1()
    p.a1()
    o.b3()
    o.a3()
    p.b2()
    o.b4()
    p.a2()
    for k in range(1, 4):
        xsend[k - 1].got()
        xshare.same(XS, (xg.at[zls[4 - k] * 2 + core], (u, sib)))
    across.append(cross(1))
    for copy in second:
        copy.wait()
    w0.w1()
    for copy in third:
        copy.wait()
    xshare.got()

    @pl.loop(0, 4)
    def _(t):
        part = pl.ds(pl.multiple_of(t * 2, 2), 2)
        rows = pl.ds(pl.multiple_of(t * BLOCK, BLOCK), BLOCK)
        project(0, rows, xg[part].reshape(BLOCK, D))

    p.b3()
    o.a4()
    o.b5()
    p.a3()
    attend_a(0, 0, 1)
    p.b4()
    attend_b(0, 0, 1)
    o1.b0()
    crossed(1)
    p1.b0()
    o1.a0()
    p1.a0()
    w0.w2()
    o.a5()
    p.a4()
    attend_a(0, 1, 1)
    o.b6()
    o1.b1()
    p.b5()
    attend_b(0, 1, 1)
    p1.b1()
    w0.w3()
    w1.w1()
    attend_b(0, 3, 1)
    o.a6()
    o1.a1()
    p1.a1()
    p.a5()
    attend_a(0, 2, 1)
    o1.b2()
    p1.b2()
    p.a6()
    attend_a(0, 3, 1)
    o1.b3()
    p1.b3()
    p.b6()
    attend_b(0, 2, 1)
    size = GROUP // CHUNKS
    halves = [pl.ds(r * size, size) for r in range(CHUNKS)]
    gsend, gshare = [], []

    def spread(r):
        own = gat.at[c, halves[r]]
        one = gat.at[0, pl.ds(0, size)]
        gsend.append([Batch(one).same(GS, (own, line(k))) for k in range(1, 4)])
        gshare.append(
            Batch(gat.at[pl.ds(0, 4), pl.ds(0, size)]).same(GS, (own, (u, sib)))
        )

    gat[c, halves[0]] = gated(halves[0])
    spread(0)
    gat[c, halves[1]] = gated(halves[1])

    def pass_on(r):
        for k in range(1, 4):
            gsend[r][k - 1].got()
            gshare[r].same(GS, (gat.at[zls[4 - k] * 2 + core, halves[r]], (u, sib)))

    def next_layer(r):
        gshare[r].got()

        @pl.loop(0, size // BLOCK)
        def _(t):
            first_row = r * size + t * BLOCK
            rows = pl.ds(pl.multiple_of(first_row, BLOCK), BLOCK)
            part = pl.ds(pl.multiple_of(r * (size // OWN) + t * 2, 2), 2)
            g = jnp.concatenate([gat[h, rows] for h in range(NC)], axis=1)
            term = jnp.dot(g, wout[0].reshape(D, D), preferred_element_type=jnp.float32)
            new = (xg[part].reshape(BLOCK, D).astype(jnp.float32) + term).astype(jnp.bfloat16)
            x1[rows, :] = new
            project(1, rows, new)

    o1.b4()
    o1.a2()
    p1.b4()
    p1.a2()
    o1.a3()
    pass_on(0)
    spread(1)
    p1.a3()
    w0.w4()
    next_layer(0)
    o1.a4()
    o1.b5()
    p1.a4()
    pass_on(1)
    p1.b5()
    next_layer(1)
    w1.w2()
    attend_a(1, 0, 1)
    attend_a(1, 1, 1)
    o1.a5()
    o1.b6()
    attend_b(1, 0, 1)
    attend_b(1, 1, 1)
    attend_b(1, 3, 1)
    w1.w3()
    p1.a5()
    attend_a(1, 2, 1)
    o1.a6()
    p1.b6()
    attend_b(1, 2, 1)
    p1.a6()
    attend_a(1, 3, 1)
    gown[...] = gated(slice(None))
    back = Batch(g1.at[pl.ds(0, NC - 1)])
    for k in range(1, NC):
        to = (c + k) % NC
        rows = pl.ds(pl.multiple_of(to * OWN, OWN), OWN)
        back.send(HS, gown.at[rows], g1.at[c], (u, to))
    mine = pl.ds(pl.multiple_of(c * OWN, OWN), OWN)
    g1[c] = gown[mine, :]
    back.got()
    w1.w4()
    g = jnp.concatenate([g1[h] for h in range(NC)], axis=1)
    term = jnp.dot(g, wout[1].reshape(D, D), preferred_element_type=jnp.float32)
    out_ref[...] = (x1[mine, :].astype(jnp.float32) + term).astype(jnp.bfloat16)
    everything = {
        AY: kva.at[:, :, pl.ds(0, 6)],
        AX: kva.at[0, 0, pl.ds(0, 7)],
        BY: kvb.at[0, 0, pl.ds(0, 3)],
        BH: kvb.at[0, 0, 0, pl.ds(0, 4)],
        BX: kvb.at[:, :, pl.ds(0, 3)],
        CA: kva.at[0, 0, 0, pl.ds(0, 2)],
        CB: kvb.at[0, 0, 0, pl.ds(0, 2)],
        XS: xg.at[pl.ds(0, 7)],
        WS: wout.at[:, pl.ds(0, 7)],
        GS: gat.at[pl.ds(0, 7)],
        HS: g1.at[pl.ds(0, 7)],
    }
    for kind, size_ref in everything.items():
        pltpu.make_async_copy(size_ref, size_ref, send_sem.at[kind]).wait()


def body(rows, weight_in, weight_out, cache, block_user, block_offset, length, count):
    bf16 = jnp.bfloat16
    hbm = pl.BlockSpec(memory_space=pl.ANY)
    return pl.pallas_call(
        kernel,
        out_shape=jax.ShapeDtypeStruct((OWN, D), bf16),
        in_specs=[hbm] * 8,
        out_specs=pl.BlockSpec(memory_space=pltpu.VMEM),
        scratch_shapes=[
            pltpu.VMEM((2, NZ, NY, NX, 2, ROWS_A, DH), bf16),
            pltpu.VMEM((2, NZ, NX, NY, 2, ROWS_B, DH), bf16),
            pltpu.VMEM((NZ, NY, NX, ROWS_A, DH), bf16),
            pltpu.VMEM((NZ, NX, NY, ROWS_B, DH), bf16),
            pltpu.VMEM((NC, OWN, D), bf16),
            pltpu.VMEM((GROUP, D), bf16),
            pltpu.VMEM((2, D, 4 * DH), bf16),
            pltpu.VMEM((2, NC, DH, D), bf16),
            pltpu.VMEM((GROUP, 2 * DH), bf16),
            pltpu.VMEM((GROUP, DH), bf16),
            pltpu.VMEM((GROUP, DH), jnp.float32),
            pltpu.VMEM((NC, GROUP, DH), bf16),
            pltpu.VMEM((GROUP, DH), bf16),
            pltpu.VMEM((NC, OWN, DH), bf16),
            pltpu.SMEM((64,), jnp.int32),
            pltpu.SMEM((64,), jnp.int32),
            pltpu.SMEM((16,), jnp.int32),
            pltpu.SMEM((16,), jnp.int32),
            pltpu.SemaphoreType.DMA((DEPARTURES,)),
            pltpu.SemaphoreType.DMA((ARRIVALS,)),
            pltpu.SemaphoreType.DMA((13,)),
        ],
        compiler_params=pltpu.CompilerParams(
            collective_id=0, has_side_effects=True, vmem_limit_bytes=60 * 1024 * 1024
        ),
        cost_estimate=pl.CostEstimate(
            flops=12_000_000_000, bytes_accessed=4_000_000, transcendentals=9_000_000
        ),
    )(
        rows,
        weight_in.reshape(2, D, 4 * DH),
        weight_out.reshape(2, DH, D),
        cache.reshape(2, 2, BLOCK, DH),
        block_user,
        block_offset,
        length,
        count,
    )


def solution(mesh):
    placed = (
        P(("users", "cand"), None),
        P(None, None, "cand", None),
        P(None, "cand", None, None),
        P(None, None, "users", "cand", None),
        P(),
        P(),
        P(),
        P(),
    )
    return jax.shard_map(
        body, mesh=mesh, in_specs=placed, out_specs=P(("users", "cand"), None), check_vma=False
    )
```
